32 devices in a mesh: col: 16 (over z, y, x), row: 2 (over core).
Axes of the slice: x: 2, y: 2, z: 4, core: 2. Of those that a mesh axis runs over, the one named last changes fastest.
Arguments:
- x_block: bfloat16 [2, 2048, 64], P('row', 'col'), may hold values from -6 to 6
- tiles: bfloat16 [16, 2, 96, 128, 128], P('col', 'row'), may hold values from -0.078125 to 0.078125
- tile_rows: int32 [16, 2, 96], P('col', 'row'), may hold values from 0 to 15
- tile_cols: int32 [16, 2, 96], P('col', 'row'), may hold values from 0 to 1
- tile_count: int32 [16, 2], P('col', 'row'), may hold values from 1 to 96, as said below
Outputs:
- filtered: bfloat16 [2, 2048, 64], P('row', 'col')
- gram: float32 [64, 64], replicated
The draws below stay inside these ranges and needn't reach their ends.
Inputs may be any that keep to these rules, and one draw needn't show every extreme that they name: `tile_count`: padding slots hold arbitrary tiles and indices; every draw has some device with all 96 slots live.
All inputs are finite; a program needn't handle non-finite values.
Results may differ from the reference program's by a relative error of at most 0.0049.
Values may be sent and summed in bfloat16 or wider, within the bound.
No kernel may reach another device: no remote copies, remote signals or barrier semaphores. Data moves between devices by JAX's collectives and lax.ppermute only.
A program may use at most 64 MiB of HBM per device.

```python
import jax
import jax.numpy as jnp
from jax import lax

KV = 64
TILES_DEV = 96
BANDS = 2
SLABS = 16
NB = 32
NDIM = 4096


def draw_tile_count(key, part):
    first_key = jax.random.fold_in(key, 11)
    second_key = jax.random.fold_in(key, 23)
    counts = jax.random.randint(first_key, (SLABS * BANDS,), 1, TILES_DEV + 1)
    chosen = jax.random.randint(second_key, (), 0, SLABS * BANDS)
    counts = jnp.where(jnp.arange(SLABS * BANDS) == chosen, TILES_DEV, counts)
    return counts.reshape(SLABS, BANDS).astype(jnp.int32)


def plant(values, stream_key, least, high):
    spot = [jax.random.randint(jax.random.fold_in(stream_key, axis), (), 0, length) for axis, length in enumerate(values.shape)]
    widest = values.shape.index(max(values.shape))
    next_to = spot[:widest] + [(spot[widest] + 1) % values.shape[widest]] + spot[widest + 1:]
    return values.at[tuple(spot)].set(least).at[tuple(next_to)].set(high)


def level_of(rng, dims, split, least, top_value):
    factor_of, own = 1.0, jax.random.fold_in(rng, 6)
    for axis_at, parts in split:
        draws = jnp.exp(jax.random.uniform(jax.random.fold_in(own, axis_at), (parts,), jnp.float32, least / len(split), top_value / len(split)))
        factor_of = factor_of * jnp.repeat(draws, dims[axis_at] // parts).reshape([-1 if axis == axis_at else 1 for axis in range(len(dims))])
    return factor_of


def bell_draw(key, extent, width, bound, cuts=(), kind=jnp.bfloat16):
    result = jax.random.normal(key, extent, jnp.float32) * width
    if len(cuts) > 0:
        result = level_of(key, extent, cuts, -0.22, 0.18) * result
    return jnp.clip(result, min=-bound, max=bound).astype(kind)


def setup_inputs(seed: int = 0) -> dict:
    arg_keys = jax.random.split(jax.random.key(seed), 6)
    x_block = bell_draw(arg_keys[0], (BANDS, SLABS * 128, KV), 1.0, 6.0, ((0, 2), (1, 16)))
    tiles = bell_draw(arg_keys[1], (SLABS, BANDS, TILES_DEV, 128, 128), (64 * TILES_DEV) ** -0.5, 0.078125, ((0, 16), (1, 2)))
    tile_rows = plant(jax.random.randint(arg_keys[2], (SLABS, BANDS, TILES_DEV), 0, SLABS), jax.random.fold_in(arg_keys[2], 1), 0, SLABS - 1).astype(jnp.int32)
    tile_cols = plant(jax.random.randint(arg_keys[3], (SLABS, BANDS, TILES_DEV), 0, BANDS), jax.random.fold_in(arg_keys[3], 1), 0, BANDS - 1).astype(jnp.int32)
    tile_count = draw_tile_count(jax.random.fold_in(arg_keys[5], 71), 0)
    return dict(x_block=x_block, tiles=tiles, tile_rows=tile_rows, tile_cols=tile_cols, tile_count=tile_count)


def apply_hamiltonian(tiles, tile_rows, tile_cols, tile_count, vec):
    slot_index = jnp.arange(TILES_DEV, dtype=jnp.int32)
    band_index = jnp.arange(BANDS, dtype=jnp.int32)

    def one_slab(acc, items):
        tile_data, rows_here, cols_here, count_here, slab_index = items
        global_cols = cols_here * SLABS + slab_index
        global_rows = band_index[:, None] * SLABS + rows_here
        live = (slot_index[None, :] < count_here[:, None]).astype(jnp.float32)
        picked = vec[global_cols.reshape(-1)].astype(jnp.float32)
        prod = jnp.einsum("tij,tjk->tik", tile_data.reshape(-1, 128, 128).astype(jnp.float32), picked)
        prod = prod * live.reshape(-1)[:, None, None]
        acc = acc + jax.ops.segment_sum(prod, global_rows.reshape(-1), NB)
        return acc, None

    start = jnp.zeros((NB, 128, KV), jnp.float32)
    slabs = jnp.arange(SLABS, dtype=jnp.int32)
    total, _ = lax.scan(one_slab, start, (tiles, tile_rows, tile_cols, tile_count, slabs))
    return total


def reference(x_block, tiles, tile_rows, tile_cols, tile_count):
    vec = x_block.reshape(NB, 128, KV)
    first = apply_hamiltonian(tiles, tile_rows, tile_cols, tile_count, vec).astype(jnp.bfloat16)
    second = apply_hamiltonian(tiles, tile_rows, tile_cols, tile_count, first)
    first_flat = first.reshape(NDIM, KV).astype(jnp.float32)
    second_flat = second.reshape(NDIM, KV)
    gram = jnp.dot(first_flat.T, second_flat, precision=lax.Precision.HIGHEST) / NDIM
    filtered = second.astype(jnp.bfloat16).reshape(BANDS, SLABS * 128, KV)
    return filtered, gram
```

```python
import functools

import jax
import jax.numpy as jnp
from jax import lax
from jax.experimental import pallas as pl
from jax.experimental.pallas import tpu as pltpu
from jax.sharding import PartitionSpec as P

F32 = jnp.float32
BF16 = jnp.bfloat16
MIB = 1 << 20


def lane_half(shape):
    return lax.broadcasted_iota(jnp.int32, shape, len(shape) - 1) // 64


def swap_halves(value):
    return pltpu.roll(value, 64, 1)


def pack(block):
    top, low = block[:64], block[64:]
    return jnp.where(lane_half(top.shape) == 0, top, swap_halves(low))


def apply_kernel(
    n_col, n_row, slots, group, rows_ref, cols_ref, count_ref, vecs_ref, tiles_ref, out_ref, staged, right, products, total, sems
):
    chunks = slots // group
    copies = [
        pltpu.make_async_copy(tiles_ref.at[0, 0, pl.ds(i * group, group)], staged.at[pl.ds(i * group, group)], sems.at[i])
        for i in range(chunks)
    ]
    for copy in copies:
        copy.start()
    lane_groups = n_row // 2
    packed = vecs_ref.shape[1] == 64
    right[...] = jnp.zeros_like(right)
    for g in range(lane_groups):
        even, odd = vecs_ref[2 * g].astype(F32), vecs_ref[2 * g + 1].astype(F32)
        if packed:
            low = lane_half(even.shape) == 0
            upper = jnp.where(low, even, swap_halves(odd))
            lower = jnp.where(low, swap_halves(even), odd)
            both = jnp.concatenate([upper, lower], axis=0)
        else:
            both = jnp.concatenate([even, odd], axis=1)
        both = both.astype(BF16)
        right[g, :128, :128] = both
        right[g, 128:, 128:] = both
    total[...] = jnp.zeros_like(total)
    half = lane_half((128, 128))
    count = count_ref[0, 0]
    for i in range(chunks):
        copies[i].wait()
        pairs = staged[pl.ds(i * group, group)].reshape(group // 2, 2, 128, 128)
        left = jnp.concatenate([pairs[:, 0], pairs[:, 1]], axis=-1).reshape(group * 64, 256)
        for g in range(lane_groups):
            products[g] = jnp.dot(left, right[g], preferred_element_type=F32)
        for j in range(group):
            slot = i * group + j
            band = cols_ref[0, 0, slot]
            place = jnp.clip(rows_ref[0, 0, slot], 0, n_col - 1)
            lane_group = jnp.clip(band // 2, 0, lane_groups - 1) if lane_groups > 1 else 0
            wanted = jnp.where(slot < count, band % 2, 2)
            term = products[lane_group, pl.ds(j // 2 * 128, 128), pl.ds(j % 2 * 128, 128)]
            total[place] += jnp.where(half == wanted, term, 0.0)
    for r in range(n_col):
        block = total[r]
        out_ref[r] = pack(block + swap_halves(block)).astype(BF16)


def apply_local(tiles, rows, cols, count, vecs, n_col):
    n_row, slots = vecs.shape[0], tiles.shape[2]
    group = next(g for g in (16, 8, 4, 2) if slots % g == 0)
    smem = pl.BlockSpec(memory_space=pltpu.SMEM)
    vmem = pl.BlockSpec(memory_space=pltpu.VMEM)
    return pl.pallas_call(
        functools.partial(apply_kernel, n_col, n_row, slots, group),
        out_shape=jax.ShapeDtypeStruct((n_col, 64, 128), BF16),
        in_specs=[smem, smem, smem, vmem, pl.BlockSpec(memory_space=pl.ANY)],
        out_specs=vmem,
        scratch_shapes=[
            pltpu.VMEM((slots, 128, 128), BF16),
            pltpu.VMEM((n_row // 2, 256, 256), BF16),
            pltpu.VMEM((n_row // 2, group * 64, 256), F32),
            pltpu.VMEM((n_col, 128, 128), F32),
            pltpu.SemaphoreType.DMA((slots // group,)),
        ],
        compiler_params=pltpu.CompilerParams(vmem_limit_bytes=32 * MIB),
        cost_estimate=pl.CostEstimate(flops=slots * 128 * 128 * 128, bytes_accessed=slots * 128 * 256, transcendentals=0),
        name="tile_products",
    )(rows, cols, count, vecs, tiles)


def sum_kernel(parts_ref, out_ref):
    out_ref[...] = jnp.sum(parts_ref[...].astype(F32), axis=0).astype(BF16)


def sum_parts(parts):
    return pl.pallas_call(
        sum_kernel, out_shape=jax.ShapeDtypeStruct(parts.shape[1:], BF16), name="sum_parts"
    )(parts)


def gram_kernel(copies, parts_ref, first_ref, filtered_ref, terms_ref):
    second = jnp.sum(parts_ref[...].astype(F32), axis=0)
    filtered_ref[0, :64, :] = second[:, :64].astype(BF16)
    filtered_ref[0, 64:, :] = swap_halves(second)[:, :64].astype(BF16)
    first = first_ref[...]
    high = second.astype(BF16)
    low = (second - high.astype(F32)).astype(BF16)
    dims = (((0,), (0,)), ((), ()))
    full = lax.dot_general(first, high, dims, preferred_element_type=F32)
    full += lax.dot_general(first, low, dims, preferred_element_type=F32)
    term = full[:64] + swap_halves(full[64:])
    term = jnp.where(lane_half((32, 128)) == 0, term[:32], swap_halves(term[32:])).astype(BF16)
    for i in range(copies):
        terms_ref[i] = term


def gram_term(parts, first, copies):
    return pl.pallas_call(
        functools.partial(gram_kernel, copies),
        out_shape=(
            jax.ShapeDtypeStruct((1, 128, 64), BF16),
            jax.ShapeDtypeStruct((copies, 32, 128), BF16),
        ),
        name="gram_term",
    )(parts, first)


def gram_sum_kernel(scale, terms_ref, out_ref):
    total = jnp.sum(terms_ref[...].astype(F32), axis=0) * scale
    out_ref[:32] = total[:, :64]
    out_ref[32:] = swap_halves(total)[:, :64]


def gram_sum(terms, scale):
    return pl.pallas_call(
        functools.partial(gram_sum_kernel, scale), out_shape=jax.ShapeDtypeStruct((64, 64), F32), name="gram_sum"
    )(terms)


def local(x_block, tiles, tile_rows, tile_cols, tile_count):
    n_col = lax.axis_size("col")
    n_row = lax.axis_size("row")

    def apply_owned(vecs):
        bands = lax.all_gather(vecs, "row", axis=0, tiled=True)
        partial = apply_local(tiles, tile_rows, tile_cols, tile_count, bands, n_col)
        return lax.all_to_all(partial, "col", 0, 0, tiled=True)

    first = sum_parts(apply_owned(x_block))
    filtered, terms = gram_term(apply_owned(first[None]), first, n_col * n_row)
    terms = lax.all_to_all(terms, ("col", "row"), 0, 0, tiled=True)
    return filtered, gram_sum(terms, 1.0 / (n_col * n_row * 128))


def solution(mesh):
    placed = (
        P("row", "col", None),
        P("col", "row", None, None, None),
        P("col", "row", None),
        P("col", "row", None),
        P("col", "row"),
    )
    return jax.shard_map(
        local, mesh=mesh, in_specs=placed, out_specs=(P("row", "col", None), P()), check_vma=False
    )
```

```python
import functools
import math

import jax
import jax.numpy as jnp
from jax import lax
from jax.experimental import pallas as pl
from jax.experimental.pallas import tpu as pltpu
from jax.sharding import PartitionSpec as P

F32 = jnp.float32
BF16 = jnp.bfloat16
MIB = 1 << 20
SMEM = pl.BlockSpec(memory_space=pltpu.SMEM)
VMEM = pl.BlockSpec(memory_space=pltpu.VMEM)
ANY = pl.BlockSpec(memory_space=pl.ANY)


def low_lanes(shape):
    return lax.broadcasted_iota(jnp.int32, shape, len(shape) - 1) < 64


def swap_halves(value):
    return pltpu.roll(value, 64, 1)


def call(kernel, out_shape, in_specs, out_specs, scratch=(), mib=4, flops=0, size=0, **kwargs):
    return pl.pallas_call(
        kernel,
        out_shape=out_shape,
        in_specs=in_specs,
        out_specs=out_specs,
        scratch_shapes=list(scratch),
        compiler_params=pltpu.CompilerParams(vmem_limit_bytes=mib * MIB),
        cost_estimate=pl.CostEstimate(flops=flops, bytes_accessed=size, transcendentals=0),
        **kwargs,
    )


def stage_kernel(n_col, n_row, group, own_first, tiles_ref, rows_ref, cols_ref, count_ref, staged_ref, info_ref, rows, cols, count, sems):
    slots = staged_ref.shape[0]
    small = [
        pltpu.make_async_copy(source, target, sems.at[i])
        for i, (source, target) in enumerate(((rows_ref, rows), (cols_ref, cols), (count_ref, count)))
    ]
    large = [
        pltpu.make_async_copy(tiles_ref.at[0, 0, pl.ds(i * group, group)], staged_ref.at[pl.ds(i * group, group)], sems.at[3 + i])
        for i in range(slots // group)
    ]
    for copy in small + large:
        copy.start()
    for copy in small:
        copy.wait()
    slot = lax.broadcasted_iota(jnp.int32, (1, slots), 1)
    band = jnp.clip(cols[0], 0, n_row - 1)
    if own_first:
        band = lax.rem(band + n_row - lax.axis_index("row"), n_row)
    info_ref[0:1] = jnp.where(slot < count[...], jnp.clip(rows[0], 0, n_col - 1), n_col)
    info_ref[1:2] = band
    for copy in large:
        copy.wait()


def stage(tiles, rows, cols, count, n_col, n_row, own_first):
    slots = tiles.shape[2]
    group = math.gcd(slots, 16)
    tiles, rows, cols = (pltpu.with_memory_space_constraint(a, pltpu.HBM) for a in (tiles, rows, cols))
    return call(
        functools.partial(stage_kernel, n_col, n_row, group, own_first),
        (pltpu.VMEM((slots, 128, 128), BF16), jax.ShapeDtypeStruct((2, slots), jnp.int32)),
        [ANY] * 4,
        (VMEM, VMEM),
        [
            pltpu.VMEM(rows.shape, jnp.int32),
            pltpu.VMEM(cols.shape, jnp.int32),
            pltpu.VMEM(count.shape, jnp.int32),
            pltpu.SemaphoreType.DMA((3 + slots // group,)),
        ],
        mib=8,
        size=tiles.size * 2,
        name="stage_tiles",
    )(tiles, rows, cols, count)


def place_vectors(right, band, top, low):
    lanes = slice(band * 128, band * 128 + 128)
    mask = low_lanes(top.shape)
    for row, part in ((0, top), (64, low)):
        part = jnp.where(mask, part, 0.0)
        right[row : row + 64, lanes] = part.astype(BF16)
        right[128 + row : 192 + row, lanes] = swap_halves(part).astype(BF16)


def products_kernel(n_col, n_row, group, transposed, info_ref, tiles_ref, *refs):
    vecs, (out_ref, right, total) = refs[:-3], refs[-3:]
    slots = tiles_ref.shape[0]
    blocks = [ref[b].astype(F32) for ref in vecs for b in range(ref.shape[0])]
    for band, block in enumerate(blocks):
        if transposed:
            block = jnp.concatenate([block, jnp.zeros_like(block)], axis=0).T
            place_vectors(right, band, block[:64], block[64:])
        else:
            place_vectors(right, band, block, swap_halves(block))
    total[...] = jnp.zeros_like(total)
    for start in range(0, slots, group):
        pieces = tiles_ref[pl.ds(start, group)]
        left = jnp.concatenate([pieces[:, :64], pieces[:, 64:]], axis=-1).reshape(group * 64, 256)
        products = jnp.dot(left, right[...], preferred_element_type=F32)
        for j in range(group):
            band = info_ref[1, start + j]
            term = products[j * 64 : j * 64 + 64, :128]
            for b in range(1, n_row):
                term = jnp.where(band == b, products[j * 64 : j * 64 + 64, b * 128 : b * 128 + 128], term)
            total[info_ref[0, start + j]] += term
    out_ref[...] = total[:n_col].astype(BF16)


def tile_products(info, tiles, vecs, n_col, n_row, transposed):
    slots = tiles.shape[0]
    return call(
        functools.partial(products_kernel, n_col, n_row, math.gcd(slots, 4), transposed),
        jax.ShapeDtypeStruct((n_col, 64, 128), BF16),
        [SMEM] + [VMEM] * (1 + len(vecs)),
        VMEM,
        [pltpu.VMEM((256, n_row * 128), BF16), pltpu.VMEM((n_col + 1, 64, 128), F32)],
        mib=16,
        flops=slots * 64 * 256 * n_row * 256,
        size=slots * 128 * 256,
        name="tile_products",
    )(info, tiles, *vecs)


def sum_kernel(parts_ref, out_ref):
    out_ref[0] = jnp.sum(parts_ref[...].astype(F32), axis=0).astype(BF16)


def sum_parts(parts):
    shape = (1,) + parts.shape[1:]
    return call(sum_kernel, jax.ShapeDtypeStruct(shape, BF16), [VMEM], VMEM, size=parts.size * 2, name="sum_parts")(parts)


def gram_kernel(parts_ref, first_ref, filtered_ref, terms_ref):
    second = jnp.sum(parts_ref[...].astype(F32), axis=0)
    first = first_ref[0]
    high = second.astype(BF16)
    low = (second - high.astype(F32)).astype(BF16)
    dims = (((0,), (0,)), ((), ()))
    full = lax.dot_general(first, high, dims, preferred_element_type=F32)
    full += lax.dot_general(first, low, dims, preferred_element_type=F32)
    term = full[:64] + swap_halves(full[64:])
    term = jnp.where(low_lanes((32, 128)), term[:32], swap_halves(term[32:])).astype(BF16)
    terms_ref[...] = jnp.broadcast_to(term[None], terms_ref.shape)
    filtered_ref[0] = jnp.concatenate([second, swap_halves(second)], axis=0).T[:64].astype(BF16)


def gram_terms(parts, first, copies):
    return call(
        gram_kernel,
        (jax.ShapeDtypeStruct((1, 64, 128), BF16), jax.ShapeDtypeStruct((copies, 32, 128), BF16)),
        [VMEM, VMEM],
        (VMEM, VMEM),
        mib=8,
        size=parts.size * 2,
        name="gram_terms",
    )(parts, first)


def gram_sum_kernel(scale, terms_ref, out_ref):
    total = jnp.sum(terms_ref[...].astype(F32), axis=0) * scale
    out_ref[:32] = total[:, :64]
    out_ref[32:] = swap_halves(total)[:, :64]


def gram_sum(terms, scale):
    return call(
        functools.partial(gram_sum_kernel, scale),
        jax.ShapeDtypeStruct((64, 64), F32),
        [VMEM],
        VMEM,
        mib=8,
        size=terms.size * 2,
        name="gram_sum",
    )(terms)


def local(x_block, tiles, tile_rows, tile_cols, tile_count):
    n_col = lax.axis_size("col")
    n_row = lax.axis_size("row")
    pairs = n_row == 2

    def exchange(vecs):
        if pairs:
            return vecs, lax.ppermute(vecs, "row", [(0, 1), (1, 0)])
        return (lax.all_gather(vecs, "row", axis=0, tiled=True),)

    vecs = exchange(jnp.swapaxes(x_block, 1, 2))
    staged, info = stage(tiles, tile_rows, tile_cols, tile_count, n_col, n_row, pairs)
    partial = tile_products(info, staged, vecs, n_col, n_row, True)
    first = sum_parts(lax.all_to_all(partial, "col", 0, 0, tiled=True))
    partial = tile_products(info, staged, exchange(first), n_col, n_row, False)
    parts = lax.all_to_all(partial, "col", 0, 0, tiled=True)
    filtered, terms = gram_terms(parts, first, n_col * n_row)
    terms = lax.all_to_all(terms, ("col", "row"), 0, 0, tiled=True)
    return jnp.swapaxes(filtered, 1, 2), gram_sum(terms, 1.0 / (n_col * n_row * 128))


def solution(mesh):
    placed = (
        P("row", "col", None),
        P("col", "row", None, None, None),
        P("col", "row", None),
        P("col", "row", None),
        P("col", "row"),
    )
    return jax.shard_map(
        local, mesh=mesh, in_specs=placed, out_specs=(P("row", "col", None), P()), check_vma=False
    )
```

```python
import functools
import math

import jax
import jax.numpy as jnp
from jax import lax
from jax.experimental import pallas as pl
from jax.experimental.pallas import tpu as pltpu
from jax.sharding import PartitionSpec as P

F32 = jnp.float32
BF16 = jnp.bfloat16
MIB = 1 << 20
SMEM = pl.BlockSpec(memory_space=pltpu.SMEM)
VMEM = pl.BlockSpec(memory_space=pltpu.VMEM)
ANY = pl.BlockSpec(memory_space=pl.ANY)


def low_lanes(shape):
    return lax.broadcasted_iota(jnp.int32, shape, len(shape) - 1) < 64


def swap_halves(value):
    return pltpu.roll(value, 64, 1)


def call(kernel, out_shape, in_specs, out_specs, scratch=(), mib=4, flops=0, size=0, **kwargs):
    return pl.pallas_call(
        kernel,
        out_shape=out_shape,
        in_specs=in_specs,
        out_specs=out_specs,
        scratch_shapes=list(scratch),
        compiler_params=pltpu.CompilerParams(vmem_limit_bytes=mib * MIB),
        cost_estimate=pl.CostEstimate(flops=flops, bytes_accessed=size, transcendentals=0),
        **kwargs,
    )


def stage_kernel(n_col, n_row, group, own_first, tiles_ref, rows_ref, cols_ref, count_ref, staged_ref, info_ref, rows, cols, count, sems):
    slots = staged_ref.shape[0]
    small = [
        pltpu.make_async_copy(source, target, sems.at[i])
        for i, (source, target) in enumerate(((rows_ref, rows), (cols_ref, cols), (count_ref, count)))
    ]
    large = [
        pltpu.make_async_copy(tiles_ref.at[0, 0, pl.ds(i * group, group)], staged_ref.at[pl.ds(i * group, group)], sems.at[3 + i])
        for i in range(slots // group)
    ]
    for copy in small + large:
        copy.start()
    for copy in small:
        copy.wait()
    slot = lax.broadcasted_iota(jnp.int32, (1, slots), 1)
    band = jnp.clip(cols[0], 0, n_row - 1)
    if own_first:
        band = lax.rem(band + n_row - lax.axis_index("row"), n_row)
    info_ref[0:1] = jnp.where(slot < count[...], jnp.clip(rows[0], 0, n_col - 1), n_col)
    info_ref[1:2] = band
    for copy in large:
        copy.wait()


def stage(tiles, rows, cols, count, n_col, n_row, own_first):
    slots = tiles.shape[2]
    group = math.gcd(slots, 16)
    tiles, rows, cols = (pltpu.with_memory_space_constraint(a, pltpu.HBM) for a in (tiles, rows, cols))
    return call(
        functools.partial(stage_kernel, n_col, n_row, group, own_first),
        (pltpu.VMEM((slots, 128, 128), BF16), jax.ShapeDtypeStruct((2, slots), jnp.int32)),
        [ANY] * 4,
        (VMEM, VMEM),
        [
            pltpu.VMEM(rows.shape, jnp.int32),
            pltpu.VMEM(cols.shape, jnp.int32),
            pltpu.VMEM(count.shape, jnp.int32),
            pltpu.SemaphoreType.DMA((3 + slots // group,)),
        ],
        mib=8,
        size=tiles.size * 2,
        name="stage_tiles",
    )(tiles, rows, cols, count)


def place_vectors(right, band, top, low):
    lanes = slice(band * 128, band * 128 + 128)
    mask = low_lanes(top.shape)
    for row, part in ((0, top), (64, low)):
        part = jnp.where(mask, part, 0.0)
        right[row : row + 64, lanes] = part.astype(BF16)
        right[128 + row : 192 + row, lanes] = swap_halves(part).astype(BF16)


def products_kernel(order, n_row, group, transposed, info_ref, tiles_ref, *refs):
    vecs, (out_ref, right, total) = refs[:-3], refs[-3:]
    slots = tiles_ref.shape[0]
    blocks = [ref[b].astype(F32) for ref in vecs for b in range(ref.shape[0])]
    for band, block in enumerate(blocks):
        if transposed:
            block = jnp.concatenate([block, jnp.zeros_like(block)], axis=0).T
            place_vectors(right, band, block[:64], block[64:])
        else:
            place_vectors(right, band, block, swap_halves(block))
    total[...] = jnp.zeros_like(total)
    for start in range(0, slots, group):
        pieces = tiles_ref[pl.ds(start, group)]
        left = jnp.concatenate([pieces[:, :64], pieces[:, 64:]], axis=-1).reshape(group * 64, 256)
        products = jnp.dot(left, right[...], preferred_element_type=F32)
        for j in range(group):
            band = info_ref[1, start + j]
            term = products[j * 64 : j * 64 + 64, :128]
            for b in range(1, n_row):
                term = jnp.where(band == b, products[j * 64 : j * 64 + 64, b * 128 : b * 128 + 128], term)
            total[info_ref[0, start + j]] += term
    for i, place in enumerate(order):
        out_ref[i] = total[place].astype(BF16)


def tile_products(info, tiles, vecs, order, n_row, transposed):
    slots, n_col = tiles.shape[0], len(order)
    return call(
        functools.partial(products_kernel, order, n_row, math.gcd(slots, 4), transposed),
        jax.ShapeDtypeStruct((n_col, 64, 128), BF16),
        [SMEM] + [VMEM] * (1 + len(vecs)),
        VMEM,
        [pltpu.VMEM((256, n_row * 128), BF16), pltpu.VMEM((n_col + 1, 64, 128), F32)],
        mib=16,
        flops=slots * 64 * 256 * n_row * 256,
        size=slots * 128 * 256,
        name="tile_products",
    )(info, tiles, *vecs)


def sum_kernel(parts_ref, out_ref):
    out_ref[0] = jnp.sum(parts_ref[...].astype(F32), axis=0).astype(BF16)


def sum_parts(parts):
    shape = (1,) + parts.shape[1:]
    return call(sum_kernel, jax.ShapeDtypeStruct(shape, BF16), [VMEM], VMEM, size=parts.size * 2, name="sum_parts")(parts)


def gram_kernel(parts_ref, first_ref, filtered_ref, term_ref):
    second = jnp.sum(parts_ref[...].astype(F32), axis=0)
    first = first_ref[0]
    high = second.astype(BF16)
    low = (second - high.astype(F32)).astype(BF16)
    dims = (((0,), (0,)), ((), ()))
    full = lax.dot_general(first, high, dims, preferred_element_type=F32)
    full += lax.dot_general(first, low, dims, preferred_element_type=F32)
    term = full[:64] + swap_halves(full[64:])
    term_ref[0] = jnp.where(low_lanes((32, 128)), term[:32], swap_halves(term[32:]))
    filtered_ref[0] = jnp.concatenate([second, swap_halves(second)], axis=0).T[:64].astype(BF16)


def gram_term(parts, first):
    return call(
        gram_kernel,
        (jax.ShapeDtypeStruct((1, 64, 128), BF16), jax.ShapeDtypeStruct((1, 32, 128), F32)),
        [VMEM, VMEM],
        (VMEM, VMEM),
        mib=8,
        size=parts.size * 2,
        name="gram_term",
    )(parts, first)


def pair_kernel(*refs):
    terms, out_ref = refs[:-1], refs[-1]
    total = sum(jnp.sum(ref[...], axis=0) for ref in terms)
    out_ref[...] = jnp.broadcast_to(total.astype(BF16)[None], out_ref.shape)


def chip_terms(terms, copies):
    return call(
        pair_kernel, jax.ShapeDtypeStruct((copies, 32, 128), BF16), [VMEM] * len(terms), VMEM, mib=8, name="chip_terms"
    )(*terms)


def gram_sum_kernel(scale, terms_ref, out_ref):
    total = jnp.sum(terms_ref[...].astype(F32), axis=0) * scale
    out_ref[:32] = total[:, :64]
    out_ref[32:] = swap_halves(total)[:, :64]


def gram_sum(terms, scale):
    return call(
        functools.partial(gram_sum_kernel, scale),
        jax.ShapeDtypeStruct((64, 64), F32),
        [VMEM],
        VMEM,
        mib=8,
        size=terms.size * 2,
        name="gram_sum",
    )(terms)


def local(x_block, tiles, tile_rows, tile_cols, tile_count):
    n_col = lax.axis_size("col")
    n_row = lax.axis_size("row")
    pairs = n_row == 2

    def exchange(vecs):
        if pairs:
            return vecs, lax.ppermute(vecs, "row", [(0, 1), (1, 0)])
        return (lax.all_gather(vecs, "row", axis=0, tiled=True),)

    order = [(i + n_col // 4) % n_col for i in range(n_col)]

    def scatter(blocks):
        return lax.all_to_all(blocks, "col", 0, 0, tiled=True, axis_index_groups=[order])

    vecs = exchange(jnp.swapaxes(x_block, 1, 2))
    staged, info = stage(tiles, tile_rows, tile_cols, tile_count, n_col, n_row, pairs)
    first = sum_parts(scatter(tile_products(info, staged, vecs, order, n_row, True)))
    parts = scatter(tile_products(info, staged, exchange(first), order, n_row, False))
    filtered, term = gram_term(parts, first)
    terms = scatter(chip_terms(exchange(term), n_col))
    return jnp.swapaxes(filtered, 1, 2), gram_sum(terms, 1.0 / (n_col * n_row * 128))


def solution(mesh):
    placed = (
        P("row", "col", None),
        P("col", "row", None, None, None),
        P("col", "row", None),
        P("col", "row", None),
        P("col", "row"),
    )
    return jax.shard_map(
        local, mesh=mesh, in_specs=placed, out_specs=(P("row", "col", None), P()), check_vma=False
    )
```

```python
import functools
import math

import jax
import jax.numpy as jnp
from jax import lax
from jax.experimental import pallas as pl
from jax.experimental.pallas import tpu as pltpu
from jax.sharding import PartitionSpec as P

F32 = jnp.float32
BF16 = jnp.bfloat16
MIB = 1 << 20
SMEM = pl.BlockSpec(memory_space=pltpu.SMEM)
VMEM = pl.BlockSpec(memory_space=pltpu.VMEM)
ANY = pl.BlockSpec(memory_space=pl.ANY)


def low_lanes(shape):
    return lax.broadcasted_iota(jnp.int32, shape, len(shape) - 1) < 64


def swap_halves(value):
    return pltpu.roll(value, 64, 1)


def in_hbm(*arrays):
    return tuple(pltpu.with_memory_space_constraint(array, pltpu.HBM) for array in arrays)


def call(kernel, out_shape, in_specs, out_specs, scratch=(), mib=4, flops=0, size=0, **kwargs):
    return pl.pallas_call(
        kernel,
        out_shape=out_shape,
        in_specs=in_specs,
        out_specs=out_specs,
        scratch_shapes=list(scratch),
        compiler_params=pltpu.CompilerParams(vmem_limit_bytes=mib * MIB),
        cost_estimate=pl.CostEstimate(flops=flops, bytes_accessed=size, transcendentals=0),
        **kwargs,
    )


def place_vectors(right, band, top, low):
    lanes = slice(band * 128, band * 128 + 128)
    mask = low_lanes(top.shape)
    for row, part in ((0, top), (64, low)):
        part = jnp.where(mask, part, 0.0)
        right[row : row + 64, lanes] = part.astype(BF16)
        right[128 + row : 192 + row, lanes] = swap_halves(part).astype(BF16)


def stage_kernel(x_ref, rows_ref, cols_ref, tiles_ref, vecs_ref, slot_rows, slot_cols, staged_ref, sems):
    pairs = ((tiles_ref.at[0, 0], staged_ref), (rows_ref, slot_rows), (cols_ref, slot_cols), (x_ref, vecs_ref))
    copies = [pltpu.make_async_copy(source, target, sems.at[i]) for i, (source, target) in enumerate(pairs)]
    for copy in copies:
        copy.start()
    for copy in copies:
        copy.wait()


def stage(x, rows, cols, tiles):
    x, rows, cols, tiles = in_hbm(x, rows, cols, tiles)
    return call(
        stage_kernel,
        (
            pltpu.VMEM(x.shape, x.dtype),
            pltpu.SMEM(rows.shape, rows.dtype),
            pltpu.SMEM(cols.shape, cols.dtype),
            pltpu.VMEM(tiles.shape[2:], tiles.dtype),
        ),
        [ANY] * 4,
        (VMEM, SMEM, SMEM, VMEM),
        [pltpu.SemaphoreType.DMA((4,))],
        size=tiles.size * 2,
        name="stage",
    )(x, rows, cols, tiles)


def spread_vectors(right, vecs, transposed):
    blocks = [ref[b].astype(F32) for ref in vecs for b in range(ref.shape[0])]
    for band, block in enumerate(blocks):
        if transposed:
            block = jnp.concatenate([block, jnp.zeros_like(block)], axis=0).T
            place_vectors(right, band, block[:64], block[64:])
        else:
            place_vectors(right, band, block, swap_halves(block))


def add_products(tiles_ref, rows, cols, count, first_band, right, total):
    n_col, n_row, slots = total.shape[0] - 1, right.shape[1] // 128, tiles_ref.shape[0]
    group = math.gcd(slots, 4)
    for start in range(0, slots, group):
        pieces = tiles_ref[pl.ds(start, group)]
        left = jnp.concatenate([pieces[:, :64], pieces[:, 64:]], axis=-1).reshape(group * 64, 256)
        products = jnp.dot(left, right[...], preferred_element_type=F32)
        for j in range(group):
            band = jnp.clip(cols[0, 0, start + j], 0, n_row - 1)
            band = jnp.where(band >= first_band, band - first_band, band + n_row - first_band)
            place = jnp.where(start + j < count, jnp.clip(rows[0, 0, start + j], 0, n_col - 1), n_col)
            term = products[j * 64 : j * 64 + 64, :128]
            for b in range(1, n_row):
                term = jnp.where(band == b, products[j * 64 : j * 64 + 64, b * 128 : b * 128 + 128], term)
            total[place] += term


def write_blocks(out_ref, total, order):
    for i, place in enumerate(order):
        out_ref[i] = total[place].astype(BF16)


def products_kernel(order, own_first, transposed, rows, cols, count_ref, tiles_ref, *refs):
    vecs, (out_ref, right, total) = refs[:-3], refs[-3:]
    first_band = lax.axis_index("row") if own_first else 0
    spread_vectors(right, vecs, transposed)
    total[...] = jnp.zeros_like(total)
    add_products(tiles_ref, rows, cols, count_ref[0, 0], first_band, right, total)
    for i, place in enumerate(order):
        out_ref[i] = total[place].astype(BF16)


def tile_products(rows, cols, count, tiles, vecs, order, n_row, own_first, transposed):
    n_col, slots = len(order), tiles.shape[0]
    return call(
        functools.partial(products_kernel, order, own_first, transposed),
        jax.ShapeDtypeStruct((n_col, 64, 128), BF16),
        [SMEM] * 3 + [VMEM] * (1 + len(vecs)),
        VMEM,
        [pltpu.VMEM((256, n_row * 128), BF16), pltpu.VMEM((n_col + 1, 64, 128), F32)],
        mib=12,
        flops=slots * 64 * 256 * n_row * 256,
        size=slots * 128 * 256,
        name="tile_products",
    )(rows, cols, count, tiles, *vecs)


def sum_kernel(parts_ref, out_ref):
    out_ref[0] = jnp.sum(parts_ref[...].astype(F32), axis=0).astype(BF16)


def sum_parts(parts):
    shape = (1,) + parts.shape[1:]
    return call(sum_kernel, jax.ShapeDtypeStruct(shape, BF16), [VMEM], VMEM, size=parts.size * 2, name="sum_parts")(parts)


def gram_kernel(parts_ref, first_ref, term_ref):
    second = jnp.sum(parts_ref[...].astype(F32), axis=0)
    first = first_ref[0]
    high = second.astype(BF16)
    low = (second - high.astype(F32)).astype(BF16)
    dims = (((0,), (0,)), ((), ()))
    full = lax.dot_general(first, high, dims, preferred_element_type=F32)
    full += lax.dot_general(first, low, dims, preferred_element_type=F32)
    term = full[:64] + swap_halves(full[64:])
    term_ref[0] = jnp.where(low_lanes((32, 128)), term[:32], swap_halves(term[32:]))


def gram_term(parts, first):
    shape = jax.ShapeDtypeStruct((1, 32, 128), F32)
    return call(gram_kernel, shape, [VMEM, VMEM], VMEM, size=parts.size * 2, name="gram_term")(parts, first)


def filtered_kernel(parts_ref, out_ref):
    second = jnp.sum(parts_ref[...].astype(F32), axis=0)
    out_ref[0] = jnp.concatenate([second, swap_halves(second)], axis=0).T[:64].astype(BF16)


def filtered_block(parts):
    shape = jax.ShapeDtypeStruct((1, 64, 128), BF16)
    return call(filtered_kernel, shape, [VMEM], VMEM, size=parts.size * 2, name="filtered_block")(parts)


def pair_kernel(*refs):
    terms, out_ref = refs[:-2], refs[-1]
    total = sum(jnp.sum(ref[...], axis=0) for ref in terms)
    out_ref[...] = jnp.broadcast_to(total.astype(BF16)[None], out_ref.shape)


def chip_terms(terms, before, copies):
    shape = jax.ShapeDtypeStruct((copies, 32, 128), BF16)
    return call(pair_kernel, shape, [VMEM] * len(terms) + [ANY], VMEM, name="chip_terms")(*terms, *in_hbm(before))


def gram_sum_kernel(scale, terms_ref, out_ref):
    total = jnp.sum(terms_ref[...].astype(F32), axis=0) * scale
    out_ref[:32] = total[:, :64]
    out_ref[32:] = swap_halves(total)[:, :64]


def gram_sum(terms, scale):
    return call(
        functools.partial(gram_sum_kernel, scale),
        jax.ShapeDtypeStruct((64, 64), F32),
        [VMEM],
        VMEM,
        mib=8,
        size=terms.size * 2,
        name="gram_sum",
    )(terms)


def local(x_block, tiles, tile_rows, tile_cols, tile_count):
    n_col = lax.axis_size("col")
    n_row = lax.axis_size("row")
    pairs = n_row == 2

    def exchange(vecs):
        if pairs:
            return vecs, lax.ppermute(vecs, "row", [(0, 1), (1, 0)])
        return (lax.all_gather(vecs, "row", axis=0, tiled=True),)

    lead = n_col * 3 // 4 - 1
    order = sorted(range(n_col), key=lambda k: k ^ lead)

    def scatter(blocks):
        return lax.all_to_all(blocks, "col", 0, 0, tiled=True, axis_index_groups=[order])

    x_turned = jnp.swapaxes(x_block, 1, 2)
    vecs = exchange(x_turned)
    own, rows, cols, staged = stage(x_turned, tile_rows, tile_cols, tiles)
    if pairs:
        vecs = (own, vecs[1])
    partial = tile_products(rows, cols, tile_count, staged, vecs, order, n_row, pairs, True)
    first = sum_parts(scatter(partial))
    partial = tile_products(rows, cols, tile_count, staged, exchange(first), order, n_row, pairs, False)
    parts = scatter(partial)
    terms = exchange(gram_term(parts, first))
    filtered = filtered_block(parts)
    terms = scatter(chip_terms(terms, filtered, n_col))
    return jnp.swapaxes(filtered, 1, 2), gram_sum(terms, 1.0 / (n_col * n_row * 128))


def solution(mesh):
    placed = (
        P("row", "col", None),
        P("col", "row", None, None, None),
        P("col", "row", None),
        P("col", "row", None),
        P("col", "row"),
    )
    return jax.shard_map(
        local, mesh=mesh, in_specs=placed, out_specs=(P("row", "col", None), P()), check_vma=False
    )
```

```python
import functools
import math

import jax
import jax.numpy as jnp
from jax import lax
from jax.experimental import pallas as pl
from jax.experimental.pallas import tpu as pltpu
from jax.sharding import PartitionSpec as P

F32 = jnp.float32
BF16 = jnp.bfloat16
MIB = 1 << 20
SMEM = pl.BlockSpec(memory_space=pltpu.SMEM)
VMEM = pl.BlockSpec(memory_space=pltpu.VMEM)
ANY = pl.BlockSpec(memory_space=pl.ANY)


def low_lanes(shape):
    return lax.broadcasted_iota(jnp.int32, shape, len(shape) - 1) < 64


def swap_halves(value):
    return pltpu.roll(value, 64, 1)


def in_hbm(*arrays):
    return tuple(pltpu.with_memory_space_constraint(array, pltpu.HBM) for array in arrays)


def call(kernel, out_shape, in_specs, out_specs, scratch=(), mib=4, flops=0, size=0, **kwargs):
    return pl.pallas_call(
        kernel,
        out_shape=out_shape,
        in_specs=in_specs,
        out_specs=out_specs,
        scratch_shapes=list(scratch),
        compiler_params=pltpu.CompilerParams(vmem_limit_bytes=mib * MIB),
        cost_estimate=pl.CostEstimate(flops=flops, bytes_accessed=size, transcendentals=0),
        **kwargs,
    )


def place_vectors(right, band, top, low):
    lanes = slice(band * 128, band * 128 + 128)
    mask = low_lanes(top.shape)
    for row, part in ((0, top), (64, low)):
        part = jnp.where(mask, part, 0.0)
        right[row : row + 64, lanes] = part.astype(BF16)
        right[128 + row : 192 + row, lanes] = swap_halves(part).astype(BF16)


def stage_kernel(x_ref, rows_ref, cols_ref, vecs_ref, slot_rows, slot_cols, sems):
    pairs = ((rows_ref, slot_rows), (cols_ref, slot_cols), (x_ref, vecs_ref))
    copies = [pltpu.make_async_copy(source, target, sems.at[i]) for i, (source, target) in enumerate(pairs)]
    for copy in copies:
        copy.start()
    for copy in copies:
        copy.wait()


def stage(x, rows, cols):
    x, rows, cols = in_hbm(x, rows, cols)
    return call(
        stage_kernel,
        (pltpu.VMEM(x.shape, x.dtype), pltpu.SMEM(rows.shape, rows.dtype), pltpu.SMEM(cols.shape, cols.dtype)),
        [ANY] * 3,
        (VMEM, SMEM, SMEM),
        [pltpu.SemaphoreType.DMA((3,))],
        flops=3 * 10**9,
        name="stage",
    )(x, rows, cols)


def spread_vectors(right, vecs, transposed):
    blocks = [ref[b].astype(F32) for ref in vecs for b in range(ref.shape[0])]
    for band, block in enumerate(blocks):
        if transposed:
            block = jnp.concatenate([block, jnp.zeros_like(block)], axis=0).T
            place_vectors(right, band, block[:64], block[64:])
        else:
            place_vectors(right, band, block, swap_halves(block))


def add_products(tiles_ref, rows, cols, count, first_band, right, total):
    n_col, n_row, slots = total.shape[0] - 1, right.shape[1] // 128, tiles_ref.shape[0]
    group = math.gcd(slots, 4)
    for start in range(0, slots, group):
        pieces = tiles_ref[pl.ds(start, group)]
        left = jnp.concatenate([pieces[:, :64], pieces[:, 64:]], axis=-1).reshape(group * 64, 256)
        products = jnp.dot(left, right[...], preferred_element_type=F32)
        for j in range(group):
            band = jnp.clip(cols[0, 0, start + j], 0, n_row - 1)
            band = jnp.where(band >= first_band, band - first_band, band + n_row - first_band)
            place = jnp.where(start + j < count, jnp.clip(rows[0, 0, start + j], 0, n_col - 1), n_col)
            term = products[j * 64 : j * 64 + 64, :128]
            for b in range(1, n_row):
                term = jnp.where(band == b, products[j * 64 : j * 64 + 64, b * 128 : b * 128 + 128], term)
            total[place] += term


def write_blocks(out_ref, total, order):
    for i, place in enumerate(order):
        out_ref[i] = total[place].astype(BF16)


def products_kernel(order, own_first, transposed, rows, cols, count_ref, tiles_ref, *refs):
    vecs, (out_ref, right, total) = refs[:-3], refs[-3:]
    first_band = lax.axis_index("row") if own_first else 0
    spread_vectors(right, vecs, transposed)
    total[...] = jnp.zeros_like(total)
    add_products(tiles_ref, rows, cols, count_ref[0, 0], first_band, right, total)
    for i, place in enumerate(order):
        out_ref[i] = total[place].astype(BF16)


def tile_products(rows, cols, count, tiles, vecs, order, n_row, own_first, transposed):
    n_col, slots = len(order), tiles.shape[0]
    return call(
        functools.partial(products_kernel, order, own_first, transposed),
        jax.ShapeDtypeStruct((n_col, 64, 128), BF16),
        [SMEM] * 3 + [VMEM] * (1 + len(vecs)),
        VMEM,
        [pltpu.VMEM((256, n_row * 128), BF16), pltpu.VMEM((n_col + 1, 64, 128), F32)],
        mib=12,
        flops=slots * 64 * 256 * n_row * 256,
        size=slots * 128 * 256,
        name="tile_products",
    )(rows, cols, count, tiles, *vecs)


def sum_kernel(parts_ref, out_ref):
    out_ref[0] = jnp.sum(parts_ref[...].astype(F32), axis=0).astype(BF16)


def sum_parts(parts):
    shape = (1,) + parts.shape[1:]
    return call(sum_kernel, jax.ShapeDtypeStruct(shape, BF16), [VMEM], VMEM, size=parts.size * 2, name="sum_parts")(parts)


def gram_kernel(parts_ref, first_ref, term_ref):
    second = jnp.sum(parts_ref[...].astype(F32), axis=0)
    first = first_ref[0]
    high = second.astype(BF16)
    low = (second - high.astype(F32)).astype(BF16)
    dims = (((0,), (0,)), ((), ()))
    full = lax.dot_general(first, high, dims, preferred_element_type=F32)
    full += lax.dot_general(first, low, dims, preferred_element_type=F32)
    term = full[:64] + swap_halves(full[64:])
    term_ref[0] = jnp.where(low_lanes((32, 128)), term[:32], swap_halves(term[32:]))


def gram_term(parts, first):
    shape = jax.ShapeDtypeStruct((1, 32, 128), F32)
    return call(gram_kernel, shape, [VMEM, VMEM], VMEM, size=parts.size * 2, name="gram_term")(parts, first)


def filtered_kernel(parts_ref, out_ref):
    second = jnp.sum(parts_ref[...].astype(F32), axis=0)
    out_ref[0] = jnp.concatenate([second, swap_halves(second)], axis=0).T[:64].astype(BF16)


def filtered_block(parts):
    shape = jax.ShapeDtypeStruct((1, 64, 128), BF16)
    return call(filtered_kernel, shape, [VMEM], VMEM, size=parts.size * 2, name="filtered_block")(parts)


def pair_kernel(*refs):
    terms, out_ref = refs[:-2], refs[-1]
    total = sum(jnp.sum(ref[...], axis=0) for ref in terms)
    out_ref[...] = jnp.broadcast_to(total.astype(BF16)[None], out_ref.shape)


def chip_terms(terms, before, copies):
    shape = jax.ShapeDtypeStruct((copies, 32, 128), BF16)
    return call(pair_kernel, shape, [VMEM] * len(terms) + [ANY], VMEM, name="chip_terms")(*terms, *in_hbm(before))


def gram_sum_kernel(scale, terms_ref, out_ref):
    total = jnp.sum(terms_ref[...].astype(F32), axis=0) * scale
    out_ref[:32] = total[:, :64]
    out_ref[32:] = swap_halves(total)[:, :64]


def gram_sum(terms, scale):
    return call(
        functools.partial(gram_sum_kernel, scale),
        jax.ShapeDtypeStruct((64, 64), F32),
        [VMEM],
        VMEM,
        mib=8,
        size=terms.size * 2,
        name="gram_sum",
    )(terms)


def local(x_block, tiles, tile_rows, tile_cols, tile_count):
    n_col = lax.axis_size("col")
    n_row = lax.axis_size("row")
    pairs = n_row == 2

    def exchange(vecs):
        if pairs:
            return vecs, lax.ppermute(vecs, "row", [(0, 1), (1, 0)])
        return (lax.all_gather(vecs, "row", axis=0, tiled=True),)

    lead = n_col * 3 // 4 - 1
    order = sorted(range(n_col), key=lambda k: k ^ lead)

    def scatter(blocks):
        return lax.all_to_all(blocks, "col", 0, 0, tiled=True, axis_index_groups=[order])

    x_turned = jnp.swapaxes(x_block, 1, 2)
    vecs = exchange(x_turned)
    own, rows, cols = stage(x_turned, tile_rows, tile_cols)
    staged = pltpu.with_memory_space_constraint(tiles[0, 0], pltpu.VMEM)
    if pairs:
        vecs = (own, vecs[1])
    partial = tile_products(rows, cols, tile_count, staged, vecs, order, n_row, pairs, True)
    first = sum_parts(scatter(partial))
    partial = tile_products(rows, cols, tile_count, staged, exchange(first), order, n_row, pairs, False)
    parts = scatter(partial)
    terms = exchange(gram_term(parts, first))
    filtered = filtered_block(parts)
    terms = scatter(chip_terms(terms, filtered, n_col))
    return jnp.swapaxes(filtered, 1, 2), gram_sum(terms, 1.0 / (n_col * n_row * 128))


def solution(mesh):
    placed = (
        P("row", "col", None),
        P("col", "row", None, None, None),
        P("col", "row", None),
        P("col", "row", None),
        P("col", "row"),
    )
    return jax.shard_map(
        local, mesh=mesh, in_specs=placed, out_specs=(P("row", "col", None), P()), check_vma=False
    )
```

```python
import functools
import math

import jax
import jax.numpy as jnp
from jax import lax
from jax.experimental import pallas as pl
from jax.experimental.pallas import tpu as pltpu
from jax.sharding import PartitionSpec as P

F32 = jnp.float32
BF16 = jnp.bfloat16
MIB = 1 << 20
SMEM = pl.BlockSpec(memory_space=pltpu.SMEM)
VMEM = pl.BlockSpec(memory_space=pltpu.VMEM)
ANY = pl.BlockSpec(memory_space=pl.ANY)


def low_lanes(shape):
    return lax.broadcasted_iota(jnp.int32, shape, len(shape) - 1) < 64


def swap_halves(value):
    return pltpu.roll(value, 64, 1)


def in_hbm(*arrays):
    return tuple(pltpu.with_memory_space_constraint(array, pltpu.HBM) for array in arrays)


def call(kernel, out_shape, in_specs, out_specs, scratch=(), mib=4, flops=0, size=0, **kwargs):
    return pl.pallas_call(
        kernel,
        out_shape=out_shape,
        in_specs=in_specs,
        out_specs=out_specs,
        scratch_shapes=list(scratch),
        compiler_params=pltpu.CompilerParams(vmem_limit_bytes=mib * MIB),
        cost_estimate=pl.CostEstimate(flops=flops, bytes_accessed=size, transcendentals=0),
        **kwargs,
    )


def place_vectors(right, band, top, low):
    lanes = slice(band * 128, band * 128 + 128)
    mask = low_lanes(top.shape)
    for row, part in ((0, top), (64, low)):
        part = jnp.where(mask, part, 0.0)
        right[row : row + 64, lanes] = part.astype(BF16)
        right[128 + row : 192 + row, lanes] = swap_halves(part).astype(BF16)


def stage_kernel(rows_ref, cols_ref, slot_rows, slot_cols, sems):
    pairs = ((rows_ref, slot_rows), (cols_ref, slot_cols))
    copies = [pltpu.make_async_copy(source, target, sems.at[i]) for i, (source, target) in enumerate(pairs)]
    for copy in copies:
        copy.start()
    for copy in copies:
        copy.wait()


def stage(rows, cols):
    rows, cols = in_hbm(rows, cols)
    return call(
        stage_kernel,
        (pltpu.SMEM(rows.shape, rows.dtype), pltpu.SMEM(cols.shape, cols.dtype)),
        [ANY] * 2,
        (SMEM, SMEM),
        [pltpu.SemaphoreType.DMA((3,))],
        flops=3 * 10**9,
        name="stage",
    )(rows, cols)


def spread_vectors(right, vecs, transposed):
    blocks = [ref[b].astype(F32) for ref in vecs for b in range(ref.shape[0])]
    for band, block in enumerate(blocks):
        if transposed:
            block = jnp.concatenate([block, jnp.zeros_like(block)], axis=0).T
            place_vectors(right, band, block[:64], block[64:])
        else:
            place_vectors(right, band, block, swap_halves(block))


def add_products(tiles_ref, rows, cols, count, first_band, right, total):
    n_col, n_row, slots = total.shape[0] - 1, right.shape[1] // 128, tiles_ref.shape[0]
    group = math.gcd(slots, 2)
    for start in range(0, slots, group):
        pieces = tiles_ref[pl.ds(start, group)]
        left = jnp.concatenate([pieces[:, :64], pieces[:, 64:]], axis=-1).reshape(group * 64, 256)
        products = jnp.dot(left, right[...], preferred_element_type=F32)
        for j in range(group):
            band = jnp.clip(cols[0, 0, start + j], 0, n_row - 1)
            band = jnp.where(band >= first_band, band - first_band, band + n_row - first_band)
            place = jnp.where(start + j < count, jnp.clip(rows[0, 0, start + j], 0, n_col - 1), n_col)
            term = products[j * 64 : j * 64 + 64, :128]
            for b in range(1, n_row):
                term = jnp.where(band == b, products[j * 64 : j * 64 + 64, b * 128 : b * 128 + 128], term)
            total[place] += term


def write_blocks(out_ref, total, order):
    for i, place in enumerate(order):
        out_ref[i] = total[place].astype(BF16)


def products_kernel(order, own_first, transposed, rows, cols, count_ref, tiles_ref, *refs):
    vecs, (out_ref, right, total) = refs[:-3], refs[-3:]
    first_band = lax.axis_index("row") if own_first else 0
    spread_vectors(right, vecs, transposed)
    total[...] = jnp.zeros_like(total)
    add_products(tiles_ref, rows, cols, count_ref[0, 0], first_band, right, total)
    for i, place in enumerate(order):
        out_ref[i] = total[place].astype(BF16)


def tile_products(rows, cols, count, tiles, vecs, order, n_row, own_first, transposed):
    n_col, slots = len(order), tiles.shape[0]
    return call(
        functools.partial(products_kernel, order, own_first, transposed),
        jax.ShapeDtypeStruct((n_col, 64, 128), BF16),
        [SMEM] * 3 + [VMEM] * (1 + len(vecs)),
        VMEM,
        [pltpu.VMEM((256, n_row * 128), BF16), pltpu.VMEM((n_col + 1, 64, 128), F32)],
        mib=12,
        flops=slots * 64 * 256 * n_row * 256,
        size=slots * 128 * 256,
        name="tile_products",
    )(rows, cols, count, tiles, *vecs)


def sum_kernel(parts_ref, out_ref):
    out_ref[0] = jnp.sum(parts_ref[...].astype(F32), axis=0).astype(BF16)


def sum_parts(parts):
    shape = (1,) + parts.shape[1:]
    return call(sum_kernel, jax.ShapeDtypeStruct(shape, BF16), [VMEM], VMEM, size=parts.size * 2, name="sum_parts")(parts)


def gram_kernel(parts_ref, first_ref, term_ref):
    second = jnp.sum(parts_ref[...].astype(F32), axis=0)
    first = first_ref[0]
    high = second.astype(BF16)
    low = (second - high.astype(F32)).astype(BF16)
    dims = (((0,), (0,)), ((), ()))
    full = lax.dot_general(first, high, dims, preferred_element_type=F32)
    full += lax.dot_general(first, low, dims, preferred_element_type=F32)
    term = full[:64] + swap_halves(full[64:])
    term_ref[0] = jnp.where(low_lanes((32, 128)), term[:32], swap_halves(term[32:]))


def gram_term(parts, first):
    shape = jax.ShapeDtypeStruct((1, 32, 128), F32)
    return call(gram_kernel, shape, [VMEM, VMEM], VMEM, size=parts.size * 2, name="gram_term")(parts, first)


def filtered_kernel(parts_ref, out_ref):
    second = jnp.sum(parts_ref[...].astype(F32), axis=0)
    out_ref[0] = jnp.concatenate([second, swap_halves(second)], axis=0).T[:64].astype(BF16)


def filtered_block(parts):
    shape = jax.ShapeDtypeStruct((1, 64, 128), BF16)
    return call(filtered_kernel, shape, [VMEM], VMEM, size=parts.size * 2, name="filtered_block")(parts)


def pair_kernel(*refs):
    terms, out_ref = refs[:-2], refs[-1]
    total = sum(jnp.sum(ref[...], axis=0) for ref in terms)
    out_ref[...] = jnp.broadcast_to(total.astype(BF16)[None], out_ref.shape)


def chip_terms(terms, before, copies):
    shape = jax.ShapeDtypeStruct((copies, 32, 128), BF16)
    return call(pair_kernel, shape, [VMEM] * len(terms) + [ANY], VMEM, name="chip_terms")(*terms, *in_hbm(before))


def gram_sum_kernel(scale, terms_ref, out_ref):
    total = jnp.sum(terms_ref[...].astype(F32), axis=0) * scale
    out_ref[:32] = total[:, :64]
    out_ref[32:] = swap_halves(total)[:, :64]


def gram_sum(terms, scale):
    return call(
        functools.partial(gram_sum_kernel, scale),
        jax.ShapeDtypeStruct((64, 64), F32),
        [VMEM],
        VMEM,
        mib=8,
        size=terms.size * 2,
        name="gram_sum",
    )(terms)


def local(x_block, tiles, tile_rows, tile_cols, tile_count):
    n_col = lax.axis_size("col")
    n_row = lax.axis_size("row")
    pairs = n_row == 2

    def exchange(vecs):
        if pairs:
            return vecs, lax.ppermute(vecs, "row", [(0, 1), (1, 0)])
        return (lax.all_gather(vecs, "row", axis=0, tiled=True),)

    lead = n_col * 3 // 4 - 1
    order = sorted(range(n_col), key=lambda k: k ^ lead)

    def scatter(blocks):
        return lax.all_to_all(blocks, "col", 0, 0, tiled=True, axis_index_groups=[order])

    x_turned = jnp.swapaxes(x_block, 1, 2)
    vecs = exchange(x_turned)
    rows, cols = stage(tile_rows, tile_cols)
    staged = pltpu.with_memory_space_constraint(tiles[0, 0], pltpu.VMEM)
    partial = tile_products(rows, cols, tile_count, staged, vecs, order, n_row, pairs, True)
    first = sum_parts(scatter(partial))
    partial = tile_products(rows, cols, tile_count, staged, exchange(first), order, n_row, pairs, False)
    parts = scatter(partial)
    terms = exchange(gram_term(parts, first))
    filtered = filtered_block(parts)
    terms = scatter(chip_terms(terms, filtered, n_col))
    return jnp.swapaxes(filtered, 1, 2), gram_sum(terms, 1.0 / (n_col * n_row * 128))


def solution(mesh):
    placed = (
        P("row", "col", None),
        P("col", "row", None, None, None),
        P("col", "row", None),
        P("col", "row", None),
        P("col", "row"),
    )
    return jax.shard_map(
        local, mesh=mesh, in_specs=placed, out_specs=(P("row", "col", None), P()), check_vma=False
    )
```

```python
import functools
import math

import jax
import jax.numpy as jnp
from jax import lax
from jax.experimental import pallas as pl
from jax.experimental.pallas import tpu as pltpu
from jax.sharding import PartitionSpec as P

F32 = jnp.float32
BF16 = jnp.bfloat16
MIB = 1 << 20
MEASURED_ORDER = {16: [11, 3, 13, 0, 2, 1, 5, 8, 6, 15, 4, 12, 9, 10, 14, 7]}
SMEM = pl.BlockSpec(memory_space=pltpu.SMEM)
VMEM = pl.BlockSpec(memory_space=pltpu.VMEM)
ANY = pl.BlockSpec(memory_space=pl.ANY)


def low_lanes(shape):
    return lax.broadcasted_iota(jnp.int32, shape, len(shape) - 1) < 64


def swap_halves(value):
    return pltpu.roll(value, 64, 1)


def in_hbm(*arrays):
    return tuple(pltpu.with_memory_space_constraint(array, pltpu.HBM) for array in arrays)


def call(kernel, out_shape, in_specs, out_specs, scratch=(), mib=4, flops=0, size=0, **kwargs):
    return pl.pallas_call(
        kernel,
        out_shape=out_shape,
        in_specs=in_specs,
        out_specs=out_specs,
        scratch_shapes=list(scratch),
        compiler_params=pltpu.CompilerParams(vmem_limit_bytes=mib * MIB),
        cost_estimate=pl.CostEstimate(flops=flops, bytes_accessed=size, transcendentals=0),
        **kwargs,
    )


def place_vectors(right, band, top, low):
    lanes = slice(band * 128, band * 128 + 128)
    mask = low_lanes(top.shape)
    for row, part in ((0, top), (64, low)):
        part = jnp.where(mask, part, 0.0)
        right[row : row + 64, lanes] = part.astype(BF16)
        right[128 + row : 192 + row, lanes] = swap_halves(part).astype(BF16)


def stage_kernel(rows_ref, cols_ref, slot_rows, slot_cols, sems):
    pairs = ((rows_ref, slot_rows), (cols_ref, slot_cols))
    copies = [pltpu.make_async_copy(source, target, sems.at[i]) for i, (source, target) in enumerate(pairs)]
    for copy in copies:
        copy.start()
    for copy in copies:
        copy.wait()


def stage(rows, cols):
    rows, cols = in_hbm(rows, cols)
    return call(
        stage_kernel,
        (pltpu.SMEM(rows.shape, rows.dtype), pltpu.SMEM(cols.shape, cols.dtype)),
        [ANY] * 2,
        (SMEM, SMEM),
        [pltpu.SemaphoreType.DMA((3,))],
        flops=3 * 10**9,
        name="stage",
    )(rows, cols)


def spread_vectors(right, vecs, transposed):
    blocks = [ref[b].astype(F32) for ref in vecs for b in range(ref.shape[0])]
    for band, block in enumerate(blocks):
        if transposed:
            block = jnp.concatenate([block, jnp.zeros_like(block)], axis=0).T
            place_vectors(right, band, block[:64], block[64:])
        else:
            place_vectors(right, band, block, swap_halves(block))


def add_products(tiles_ref, rows, cols, count, first_band, right, total):
    n_col, n_row, slots = total.shape[0] - 1, right.shape[1] // 128, tiles_ref.shape[0]
    group = math.gcd(slots, 2)
    for start in range(0, slots, group):
        pieces = tiles_ref[pl.ds(start, group)]
        left = jnp.concatenate([pieces[:, :64], pieces[:, 64:]], axis=-1).reshape(group * 64, 256)
        products = jnp.dot(left, right[...], preferred_element_type=F32)
        for j in range(group):
            band = jnp.clip(cols[0, 0, start + j], 0, n_row - 1)
            band = jnp.where(band >= first_band, band - first_band, band + n_row - first_band)
            place = jnp.where(start + j < count, jnp.clip(rows[0, 0, start + j], 0, n_col - 1), n_col)
            term = products[j * 64 : j * 64 + 64, :128]
            for b in range(1, n_row):
                term = jnp.where(band == b, products[j * 64 : j * 64 + 64, b * 128 : b * 128 + 128], term)
            total[place] += term


def write_blocks(out_ref, total, order):
    for i, place in enumerate(order):
        out_ref[i] = total[place].astype(BF16)


def products_kernel(order, own_first, transposed, rows, cols, count_ref, tiles_ref, *refs):
    vecs, (out_ref, right, total) = refs[:-3], refs[-3:]
    first_band = lax.axis_index("row") if own_first else 0
    spread_vectors(right, vecs, transposed)
    total[...] = jnp.zeros_like(total)
    add_products(tiles_ref, rows, cols, count_ref[0, 0], first_band, right, total)
    for i, place in enumerate(order):
        out_ref[i] = total[place].astype(BF16)


def tile_products(rows, cols, count, tiles, vecs, order, n_row, own_first, transposed):
    n_col, slots = len(order), tiles.shape[0]
    return call(
        functools.partial(products_kernel, order, own_first, transposed),
        jax.ShapeDtypeStruct((n_col, 64, 128), BF16),
        [SMEM] * 3 + [VMEM] * (1 + len(vecs)),
        VMEM,
        [pltpu.VMEM((256, n_row * 128), BF16), pltpu.VMEM((n_col + 1, 64, 128), F32)],
        mib=12,
        flops=slots * 64 * 256 * n_row * 256,
        size=slots * 128 * 256,
        name="tile_products",
    )(rows, cols, count, tiles, *vecs)


def sum_kernel(parts_ref, out_ref):
    out_ref[0] = jnp.sum(parts_ref[...].astype(F32), axis=0).astype(BF16)


def sum_parts(parts):
    shape = (1,) + parts.shape[1:]
    return call(sum_kernel, jax.ShapeDtypeStruct(shape, BF16), [VMEM], VMEM, size=parts.size * 2, name="sum_parts")(parts)


def gram_kernel(parts_ref, first_ref, term_ref):
    second = jnp.sum(parts_ref[...].astype(F32), axis=0)
    first = first_ref[0]
    high = second.astype(BF16)
    low = (second - high.astype(F32)).astype(BF16)
    dims = (((0,), (0,)), ((), ()))
    full = lax.dot_general(first, high, dims, preferred_element_type=F32)
    full += lax.dot_general(first, low, dims, preferred_element_type=F32)
    term = full[:64] + swap_halves(full[64:])
    term_ref[0] = jnp.where(low_lanes((32, 128)), term[:32], swap_halves(term[32:]))


def gram_term(parts, first):
    shape = jax.ShapeDtypeStruct((1, 32, 128), F32)
    return call(gram_kernel, shape, [VMEM, VMEM], VMEM, size=parts.size * 2, name="gram_term")(parts, first)


def filtered_kernel(parts_ref, out_ref):
    second = jnp.sum(parts_ref[...].astype(F32), axis=0)
    out_ref[0] = jnp.concatenate([second, swap_halves(second)], axis=0).T[:64].astype(BF16)


def filtered_block(parts):
    shape = jax.ShapeDtypeStruct((1, 64, 128), BF16)
    return call(filtered_kernel, shape, [VMEM], VMEM, size=parts.size * 2, name="filtered_block")(parts)


def pair_kernel(*refs):
    terms, out_ref = refs[:-2], refs[-1]
    total = sum(jnp.sum(ref[...], axis=0) for ref in terms)
    out_ref[...] = jnp.broadcast_to(total.astype(BF16)[None], out_ref.shape)


def chip_terms(terms, before, copies):
    shape = jax.ShapeDtypeStruct((copies, 32, 128), BF16)
    return call(pair_kernel, shape, [VMEM] * len(terms) + [ANY], VMEM, name="chip_terms")(*terms, *in_hbm(before))


def gram_sum_kernel(scale, terms_ref, out_ref):
    total = jnp.sum(terms_ref[...].astype(F32), axis=0) * scale
    out_ref[:32] = total[:, :64]
    out_ref[32:] = swap_halves(total)[:, :64]


def gram_sum(terms, scale):
    return call(
        functools.partial(gram_sum_kernel, scale),
        jax.ShapeDtypeStruct((64, 64), F32),
        [VMEM],
        VMEM,
        mib=8,
        size=terms.size * 2,
        name="gram_sum",
    )(terms)


def local(x_block, tiles, tile_rows, tile_cols, tile_count):
    n_col = lax.axis_size("col")
    n_row = lax.axis_size("row")
    pairs = n_row == 2

    def exchange(vecs):
        if pairs:
            return vecs, lax.ppermute(vecs, "row", [(0, 1), (1, 0)])
        return (lax.all_gather(vecs, "row", axis=0, tiled=True),)

    lead = n_col * 3 // 4 - 1
    order = MEASURED_ORDER.get(n_col, sorted(range(n_col), key=lambda k: k ^ lead))

    def scatter(blocks):
        return lax.all_to_all(blocks, "col", 0, 0, tiled=True, axis_index_groups=[order])

    x_turned = jnp.swapaxes(x_block, 1, 2)
    vecs = exchange(x_turned)
    rows, cols = stage(tile_rows, tile_cols)
    staged = pltpu.with_memory_space_constraint(tiles[0, 0], pltpu.VMEM)
    partial = tile_products(rows, cols, tile_count, staged, vecs, order, n_row, pairs, True)
    first = sum_parts(scatter(partial))
    partial = tile_products(rows, cols, tile_count, staged, exchange(first), order, n_row, pairs, False)
    parts = scatter(partial)
    terms = exchange(gram_term(parts, first))
    filtered = filtered_block(parts)
    terms = scatter(chip_terms(terms, filtered, n_col))
    return jnp.swapaxes(filtered, 1, 2), gram_sum(terms, 1.0 / (n_col * n_row * 128))


def solution(mesh):
    placed = (
        P("row", "col", None),
        P("col", "row", None, None, None),
        P("col", "row", None),
        P("col", "row", None),
        P("col", "row"),
    )
    return jax.shard_map(
        local, mesh=mesh, in_specs=placed, out_specs=(P("row", "col", None), P()), check_vma=False
    )
```

```python
import functools
import math

import jax
import jax.numpy as jnp
from jax import lax
from jax.experimental import pallas as pl
from jax.experimental.pallas import tpu as pltpu
from jax.sharding import PartitionSpec as P

F32 = jnp.float32
BF16 = jnp.bfloat16
MIB = 1 << 20
MEASURED_ORDER = {16: [11, 3, 13, 0, 2, 1, 5, 8, 6, 15, 4, 12, 9, 10, 14, 7]}
SMEM = pl.BlockSpec(memory_space=pltpu.SMEM)
VMEM = pl.BlockSpec(memory_space=pltpu.VMEM)
ANY = pl.BlockSpec(memory_space=pl.ANY)


def low_lanes(shape):
    return lax.broadcasted_iota(jnp.int32, shape, len(shape) - 1) < 64


def swap_halves(value):
    return pltpu.roll(value, 64, 1)


def in_hbm(*arrays):
    return tuple(pltpu.with_memory_space_constraint(array, pltpu.HBM) for array in arrays)


def call(kernel, out_shape, in_specs, out_specs, scratch=(), mib=4, flops=0, size=0, **kwargs):
    return pl.pallas_call(
        kernel,
        out_shape=out_shape,
        in_specs=in_specs,
        out_specs=out_specs,
        scratch_shapes=list(scratch),
        compiler_params=pltpu.CompilerParams(vmem_limit_bytes=mib * MIB),
        cost_estimate=pl.CostEstimate(flops=flops, bytes_accessed=size, transcendentals=0),
        **kwargs,
    )


def place_vectors(right, band, top, low):
    lanes = slice(band * 128, band * 128 + 128)
    mask = low_lanes(top.shape)
    for row, part in ((0, top), (64, low)):
        part = jnp.where(mask, part, 0.0)
        right[row : row + 64, lanes] = part.astype(BF16)
        right[128 + row : 192 + row, lanes] = swap_halves(part).astype(BF16)


def stage_kernel(rows_ref, cols_ref, slot_rows, slot_cols, sems):
    pairs = ((rows_ref, slot_rows), (cols_ref, slot_cols))
    copies = [pltpu.make_async_copy(source, target, sems.at[i]) for i, (source, target) in enumerate(pairs)]
    for copy in copies:
        copy.start()
    for copy in copies:
        copy.wait()


def stage(rows, cols):
    rows, cols = in_hbm(rows, cols)
    return call(
        stage_kernel,
        (pltpu.SMEM(rows.shape, rows.dtype), pltpu.SMEM(cols.shape, cols.dtype)),
        [ANY] * 2,
        (SMEM, SMEM),
        [pltpu.SemaphoreType.DMA((3,))],
        flops=3 * 10**9,
        name="stage",
    )(rows, cols)


def spread_vectors(right, vecs, transposed):
    blocks = [ref[b].astype(F32) for ref in vecs for b in range(ref.shape[0])]
    for band, block in enumerate(blocks):
        if transposed:
            block = jnp.concatenate([block, jnp.zeros_like(block)], axis=0).T
            place_vectors(right, band, block[:64], block[64:])
        else:
            place_vectors(right, band, block, swap_halves(block))


def add_products(tiles_ref, rows, cols, count, first_band, right, total):
    n_col, n_row, slots = total.shape[0] - 1, right.shape[1] // 128, tiles_ref.shape[0]
    group = math.gcd(slots, 2)
    for start in range(0, slots, group):
        pieces = tiles_ref[pl.ds(start, group)]
        left = jnp.concatenate([pieces[:, :64], pieces[:, 64:]], axis=-1).reshape(group * 64, 256)
        products = jnp.dot(left, right[...], preferred_element_type=F32)
        for j in range(group):
            band = jnp.clip(cols[0, 0, start + j], 0, n_row - 1)
            band = jnp.where(band >= first_band, band - first_band, band + n_row - first_band)
            place = jnp.where(start + j < count, jnp.clip(rows[0, 0, start + j], 0, n_col - 1), n_col)
            term = products[j * 64 : j * 64 + 64, :128]
            for b in range(1, n_row):
                term = jnp.where(band == b, products[j * 64 : j * 64 + 64, b * 128 : b * 128 + 128], term)
            total[place] += term


def write_blocks(out_ref, total, order):
    for i, place in enumerate(order):
        out_ref[i] = total[place].astype(BF16)


def products_kernel(order, own_first, transposed, rows, cols, count_ref, tiles_ref, *refs):
    vecs, (out_ref, right, total) = refs[:-3], refs[-3:]
    first_band = lax.axis_index("row") if own_first else 0
    spread_vectors(right, vecs, transposed)
    total[...] = jnp.zeros_like(total)
    add_products(tiles_ref, rows, cols, count_ref[0, 0], first_band, right, total)
    for i, place in enumerate(order):
        out_ref[i] = total[place].astype(BF16)


def tile_products(rows, cols, count, tiles, vecs, order, n_row, own_first, transposed):
    n_col, slots = len(order), tiles.shape[0]
    return call(
        functools.partial(products_kernel, order, own_first, transposed),
        jax.ShapeDtypeStruct((n_col, 64, 128), BF16),
        [SMEM] * 3 + [VMEM] * (1 + len(vecs)),
        VMEM,
        [pltpu.VMEM((256, n_row * 128), BF16), pltpu.VMEM((n_col + 1, 64, 128), F32)],
        mib=12,
        flops=slots * 64 * 256 * n_row * 256,
        size=slots * 128 * 256,
        name="tile_products",
    )(rows, cols, count, tiles, *vecs)


def sum_kernel(parts_ref, out_ref):
    out_ref[0] = jnp.sum(parts_ref[...].astype(F32), axis=0).astype(BF16)


def sum_parts(parts):
    shape = (1,) + parts.shape[1:]
    return call(sum_kernel, jax.ShapeDtypeStruct(shape, BF16), [VMEM], VMEM, size=parts.size * 2, name="sum_parts")(parts)


def gram_kernel(parts_ref, first_ref, term_ref):
    second = jnp.sum(parts_ref[...].astype(F32), axis=0)
    first = first_ref[0]
    high = second.astype(BF16)
    low = (second - high.astype(F32)).astype(BF16)
    dims = (((0,), (0,)), ((), ()))
    full = lax.dot_general(first, high, dims, preferred_element_type=F32)
    full += lax.dot_general(first, low, dims, preferred_element_type=F32)
    term = full[:64] + swap_halves(full[64:])
    term_ref[0] = jnp.where(low_lanes((32, 128)), term[:32], swap_halves(term[32:]))


def gram_term(parts, first):
    shape = jax.ShapeDtypeStruct((1, 32, 128), F32)
    return call(gram_kernel, shape, [VMEM, VMEM], VMEM, size=parts.size * 2, name="gram_term")(parts, first)


def filtered_kernel(parts_ref, out_ref):
    second = jnp.sum(parts_ref[...].astype(F32), axis=0)
    out_ref[0] = jnp.concatenate([second, swap_halves(second)], axis=0).T[:64].astype(BF16)


def filtered_block(parts):
    shape = jax.ShapeDtypeStruct((1, 64, 128), BF16)
    return call(filtered_kernel, shape, [VMEM], VMEM, size=parts.size * 2, name="filtered_block")(parts)


def pair_kernel(*refs):
    terms, out_ref = refs[:-2], refs[-1]
    total = sum(jnp.sum(ref[...], axis=0) for ref in terms)
    out_ref[...] = jnp.broadcast_to(total.astype(BF16)[None], out_ref.shape)


def chip_terms(terms, before, copies):
    shape = jax.ShapeDtypeStruct((copies, 32, 128), BF16)
    return call(pair_kernel, shape, [VMEM] * len(terms) + [ANY], VMEM, name="chip_terms")(*terms, *in_hbm(before))


def gram_sum_kernel(scale, terms_ref, out_ref):
    total = jnp.sum(terms_ref[...].astype(F32), axis=0) * scale
    out_ref[:32] = total[:, :64]
    out_ref[32:] = swap_halves(total)[:, :64]


def gram_sum(terms, scale):
    return call(
        functools.partial(gram_sum_kernel, scale),
        jax.ShapeDtypeStruct((64, 64), F32),
        [VMEM],
        VMEM,
        mib=8,
        size=terms.size * 2,
        name="gram_sum",
    )(terms)


def local(x_block, tiles, tile_rows, tile_cols, tile_count):
    n_col = lax.axis_size("col")
    n_row = lax.axis_size("row")
    pairs = n_row == 2

    def exchange(vecs):
        if pairs:
            return vecs, lax.ppermute(vecs, "row", [(0, 1), (1, 0)])
        return (lax.all_gather(vecs, "row", axis=0, tiled=True),)

    lead = n_col * 3 // 4 - 1
    order = MEASURED_ORDER.get(n_col, sorted(range(n_col), key=lambda k: k ^ lead))

    def scatter(blocks, order=order):
        return lax.all_to_all(blocks, "col", 0, 0, tiled=True, axis_index_groups=[order])

    x_turned = jnp.swapaxes(x_block, 1, 2)
    vecs = exchange(x_turned)
    rows, cols = stage(tile_rows, tile_cols)
    staged = pltpu.with_memory_space_constraint(tiles[0, 0], pltpu.VMEM)
    partial = tile_products(rows, cols, tile_count, staged, vecs, order, n_row, pairs, True)
    first = sum_parts(scatter(partial))
    partial = tile_products(rows, cols, tile_count, staged, exchange(first), order, n_row, pairs, False)
    parts = scatter(partial)
    terms = exchange(gram_term(parts, first))
    filtered = filtered_block(parts)
    gram_order = sorted(range(n_col), key=lambda k: k ^ lead)
    terms = scatter(chip_terms(terms, filtered, n_col), gram_order)
    return jnp.swapaxes(filtered, 1, 2), gram_sum(terms, 1.0 / (n_col * n_row * 128))


def solution(mesh):
    placed = (
        P("row", "col", None),
        P("col", "row", None, None, None),
        P("col", "row", None),
        P("col", "row", None),
        P("col", "row"),
    )
    return jax.shard_map(
        local, mesh=mesh, in_specs=placed, out_specs=(P("row", "col", None), P()), check_vma=False
    )
```
